32 devices in a mesh: seq: 8 (over z, core), head: 4 (over y, x).
Axes of the slice: x: 2, y: 2, z: 4, core: 2. Of those that a mesh axis runs over, the one named last changes fastest.
Arguments:
- projections: bfloat16 [6144, 8, 384], P(('seq', 'head')), may hold values from -8 to 8
- routed_heads: int32 [6144, 8], P(('seq', 'head')), may hold values from 0 to 63, as said below
- slot_index: int32 [6144, 8], P(('seq', 'head')), may hold values from 0 to 47, as said below
- gate_logits: float32 [6144, 8], P(('seq', 'head')), may hold values from -8 to 8
- doc_lengths: int32 [16], replicated, may hold values from 1 to 768, 6144 in all
- cotangent: bfloat16 [6144, 8, 128], P(('seq', 'head')), may hold values from -6 to 6
Outputs:
- head_outputs: bfloat16 [6144, 8, 128], P(('seq', 'head'))
- projection_grads: bfloat16 [6144, 8, 384], P(('seq', 'head'))
- gate_grads: float32 [6144, 8], P(('seq', 'head'))
The draws below stay inside these ranges and needn't reach their ends.
Inputs may be any that keep to these rules, and one draw needn't show every extreme that they name: `routed_heads`: each token names 8 different heads. Among the 192 tokens of one aligned block at most 48 name the same head, and in every aligned run of 768 tokens one head is named by exactly 48 tokens of each of its aligned blocks of 192. slot_index[t, k] is the number of tokens before t in t's aligned block of 192 tokens that name head routed_heads[t, k]. `doc_lengths`: the documents lie in order and together fill the 6144 positions.
All inputs are finite; a program needn't handle non-finite values.
Results may differ from the reference program's by a relative error of at most 0.011.
Values may be sent and summed in bfloat16 or wider, within the bound.
No kernel may reach another device: no remote copies, remote signals or barrier semaphores. Data moves between devices by JAX's collectives and lax.ppermute only.
A program may use at most 64 MiB of HBM per device.

```python
import math
from functools import partial
import jax
import jax.numpy as jnp
import numpy as np
from jax import lax

H = 64
HS = 128
TOP = 8
TOK_DEV = 192
CAP = 48
SEQ_TOK = 768
TOKENS = 6144
NDOC = 16
N_SEQ = 8
N_HEAD = 4


def lane_counts(count_key, total_rows, lane_size):
    base_rows = total_rows // lane_size
    extra_rows = total_rows % lane_size
    counts = base_rows + (jnp.arange(lane_size, dtype=jnp.int32) < extra_rows).astype(jnp.int32)
    pair_count = lane_size // 2
    shifts = jax.random.randint(count_key, (pair_count,), 0, max(base_rows, 1), dtype=jnp.int32)
    counts = counts.at[0:2 * pair_count:2].add(shifts)
    counts = counts.at[1:2 * pair_count:2].add(-shifts)
    return counts.astype(jnp.int32)


def routing(key):
    base_key = jax.random.fold_in(key, 7001)
    hot_key, offset_key, count_key, order_key, column_key = jax.random.split(base_key, 5)
    blocks = TOKENS // TOK_DEV
    groups = TOKENS // SEQ_TOK
    lane_size = H // TOP
    hot_heads = jax.random.randint(hot_key, (groups,), 0, H, dtype=jnp.int32)
    block_hot = jnp.repeat(hot_heads, SEQ_TOK // TOK_DEV)

    def block_heads(one_key):
        others = jax.random.permutation(one_key, H - 1).astype(jnp.int32) + 1
        return jnp.concatenate([jnp.zeros((1,), jnp.int32), others])
    offsets = jax.vmap(block_heads)(jax.random.split(offset_key, blocks))
    head_table = ((block_hot[:, None] + offsets) % H).reshape(blocks, TOP, lane_size)

    def block_counts(one_key):
        first_key, rest_key = jax.random.split(one_key)
        hot_lane = jnp.concatenate([jnp.full((1,), CAP, jnp.int32), lane_counts(first_key, TOK_DEV - CAP, lane_size - 1)])
        other_lanes = jax.vmap(partial(lane_counts, total_rows=TOK_DEV, lane_size=lane_size))(jax.random.split(rest_key, TOP - 1))
        return jnp.concatenate([hot_lane[None, :], other_lanes], 0)
    counts = jax.vmap(block_counts)(jax.random.split(count_key, blocks))
    order_keys = jax.random.split(order_key, blocks * TOP)
    rank_table = jax.vmap(lambda one_key: jax.random.permutation(one_key, TOK_DEV).astype(jnp.int32))(order_keys)
    rank_table = rank_table.reshape(blocks, TOP, TOK_DEV)
    bounds = jnp.cumsum(counts, axis=2)[:, :, :-1]
    lane_place = jnp.sum((rank_table[:, :, :, None] >= bounds[:, :, None, :]).astype(jnp.int32), axis=3)
    chosen = jnp.take_along_axis(head_table, lane_place, axis=2)
    same_head = lane_place[:, :, :, None] == lane_place[:, :, None, :]
    earlier = jnp.arange(TOK_DEV)[None, :] < jnp.arange(TOK_DEV)[:, None]
    slot_table = jnp.sum((same_head & earlier[None, None, :, :]).astype(jnp.int32), axis=3)
    order_scores = jax.random.randint(column_key, (blocks, TOK_DEV, TOP), 0, 1 << 16, dtype=jnp.int32) * TOP + jnp.arange(TOP, dtype=jnp.int32)
    column_order = jnp.argsort(order_scores, axis=2)
    heads_out = jnp.take_along_axis(jnp.transpose(chosen, (0, 2, 1)), column_order, axis=2)
    slots_out = jnp.take_along_axis(jnp.transpose(slot_table, (0, 2, 1)), column_order, axis=2)
    return (heads_out.reshape(TOKENS, TOP).astype(jnp.int32), slots_out.reshape(TOKENS, TOP).astype(jnp.int32))


def draw_routed_heads(key, part):
    return routing(key)[0]


def draw_slot_index(key, part):
    return routing(key)[1]


def draw_projections(key, part):
    draw_key = jax.random.fold_in(key, 9001)
    base_key = jax.random.fold_in(draw_key, 0)
    full_shape = (TOKENS, TOP, 3 * HS)
    entries = jnp.clip(jax.random.normal(base_key, full_shape, jnp.float32), -6.0, 6.0)
    return entries.astype(jnp.bfloat16)


def block_levels(rng, extent, cuts, low, high):
    def one(dim, parts):
        heights = jax.random.uniform(jax.random.fold_in(jax.random.fold_in(rng, 6), dim), (parts,), jnp.float32, low / len(cuts), high / len(cuts))
        return jnp.repeat(jnp.exp(heights), extent[dim] // parts).reshape((-1,) + (1,) * (len(extent) - dim - 1))

    loudness = one(*cuts[0])
    for cut in cuts[1:]:
        loudness = loudness * one(*cut)
    return loudness


def length_profile(count, total, limit, slope):
    portions = [(1 << 20) // math.isqrt(rank ** slope) + 1 for rank in range(2, count + 1)]
    surplus, holding = total - limit - (count - 1), [1] * (count - 1)
    while surplus > 0:
        candidates = [i for i in range(count - 1) if holding[i] < limit]
        mass, remaining = sum([portions[i] for i in candidates]), surplus
        for i in candidates:
            extra = min(limit - holding[i], max(1, remaining * portions[i] // mass), surplus)
            holding[i] = holding[i] + extra
            surplus = surplus - extra
    return np.array([limit] + holding)


def ragged(key, amount, total, bound, skew):
    if amount == 2:
        one = jax.random.randint(key, (), max(1, total - bound), min(bound, total - 1) + 1)
        return jnp.stack([one, total - one])
    sizes = jnp.asarray(length_profile(amount, total, bound, skew), jnp.int32)
    twos = (amount - 1) // 2
    donor, sink = sizes[1:1 + 2 * twos:2], sizes[2:2 + 2 * twos:2]
    slack = jnp.minimum(donor - 1, bound - sink)
    moved = jax.random.randint(jax.random.fold_in(key, 1), (twos,), 0, 1 << 20) % (slack + 1)
    sizes = sizes.at[1:1 + 2 * twos:2].set(donor - moved).at[2:2 + 2 * twos:2].set(sink + moved)
    return sizes[jax.random.permutation(jax.random.fold_in(key, 2), amount)]


def scatter_about(own_key, shape, width, limit, cuts=(), held_as=jnp.bfloat16):
    array = width * jax.random.normal(own_key, shape, jnp.float32)
    if cuts:
        array = array * block_levels(own_key, shape, cuts, -0.22, 0.18)
    return jnp.clip(array, -limit, limit).astype(held_as)


def setup_inputs(seed: int = 0) -> dict:
    streams_of = jax.random.split(jax.random.key(seed), 7)
    return {
        "projections": draw_projections(jax.random.fold_in(streams_of[6], 71), 0),
        "routed_heads": draw_routed_heads(jax.random.fold_in(streams_of[6], 71), 0),
        "slot_index": draw_slot_index(jax.random.fold_in(streams_of[6], 71), 0),
        "gate_logits": scatter_about(streams_of[3], (TOKENS, TOP), 2.0, 8.0, ((0, 32),), jnp.float32),
        "doc_lengths": ragged(streams_of[4], NDOC, TOKENS, SEQ_TOK, 1).astype(jnp.int32),
        "cotangent": scatter_about(streams_of[5], (TOKENS, TOP, HS), 1.0, 6.0, ((0, 32),)),
    }


MASKED = -1e30


def block_pass(rows_here, docs_here, rows_before, docs_before, grads_out, carried):
    head_size = grads_out.shape[1]
    slot_span = docs_here.shape[0]
    scaling = head_size ** -0.5
    queries = rows_here[:, :head_size]
    key_rows = jnp.concatenate([rows_before[:, :head_size], rows_here[:, head_size:2 * head_size]], 0)
    value_rows = jnp.concatenate([rows_before[:, head_size:], rows_here[:, 2 * head_size:]], 0)
    key_docs = jnp.concatenate([docs_before, docs_here], 0)
    row_index = jnp.arange(slot_span, dtype=jnp.int32)[:, None]
    col_index = jnp.arange(2 * slot_span, dtype=jnp.int32)[None, :]
    visible = (key_docs[None, :] == docs_here[:, None]) & (key_docs[None, :] > 0) & (col_index - slot_span <= row_index)
    scores = jnp.dot(queries, key_rows.T, preferred_element_type=jnp.float32) * scaling
    scores = jnp.where(visible, scores, MASKED)
    row_max = jnp.max(scores, axis=1, keepdims=True)
    powers = jnp.exp(scores - row_max)
    row_sum = jnp.sum(powers, axis=1, keepdims=True)
    weights = powers / row_sum
    weights_low = weights.astype(jnp.bfloat16)
    attended = jnp.dot(weights_low, value_rows, preferred_element_type=jnp.float32).astype(jnp.bfloat16)
    attended = lax.optimization_barrier(attended)
    deltas = jnp.sum(grads_out.astype(jnp.float32) * attended.astype(jnp.float32), axis=1, keepdims=True)
    weight_grads = jnp.dot(grads_out, value_rows.T, preferred_element_type=jnp.float32)
    score_grads = (weights * (weight_grads - deltas)).astype(jnp.bfloat16)
    query_grads = jnp.dot(score_grads, key_rows, preferred_element_type=jnp.float32) * scaling
    key_grads = jnp.dot(score_grads.T, queries, preferred_element_type=jnp.float32) * scaling
    value_grads = jnp.dot(weights_low.T, grads_out, preferred_element_type=jnp.float32)
    own_keys = key_grads[slot_span:] + carried[0]
    own_values = value_grads[slot_span:] + carried[1]
    gradients = jnp.concatenate([query_grads, own_keys, own_values], 1).astype(jnp.bfloat16)
    return (key_grads[:slot_span], value_grads[:slot_span]), attended, gradients


def reference(projections, routed_heads, slot_index, gate_logits, doc_lengths, cotangent):
    token_total = projections.shape[0]
    full_width = projections.shape[2]
    head_size = full_width // 3
    slot_span = N_HEAD * CAP
    positions = jnp.arange(token_total, dtype=jnp.int32)
    doc_ends = jnp.cumsum(doc_lengths).astype(jnp.int32)
    documents = jnp.sum((positions[:, None] >= doc_ends[None, :]).astype(jnp.int32), axis=1) + 1
    zero_pairs = jnp.zeros_like(routed_heads)
    seq_block = ((positions // SEQ_TOK)[:, None] + zero_pairs).astype(jnp.int32)
    placed = (((positions // TOK_DEV) % N_HEAD)[:, None] * CAP + slot_index).astype(jnp.int32)
    pair_docs = (documents[:, None] + zero_pairs).astype(jnp.int32)
    gate_values = jax.nn.sigmoid(gate_logits)
    grads_out = (cotangent.astype(jnp.float32) * gate_values[:, :, None]).astype(jnp.bfloat16)
    proj_slots = jnp.zeros((H, N_SEQ, slot_span, full_width), projections.dtype).at[routed_heads, seq_block, placed].set(projections)
    doc_slots = jnp.zeros((H, N_SEQ, slot_span), jnp.int32).at[routed_heads, seq_block, placed].set(pair_docs)
    out_slots = jnp.zeros((H, N_SEQ, slot_span, head_size), grads_out.dtype).at[routed_heads, seq_block, placed].set(grads_out)

    def one_head(operands):
        rows_all, docs_all, outs_all = operands
        rows_before = jnp.concatenate([jnp.zeros_like(rows_all[:1, :, head_size:]), rows_all[:-1, :, head_size:]], 0)
        docs_before = jnp.concatenate([jnp.zeros_like(docs_all[:1]), docs_all[:-1]], 0)

        def advance(carried, inputs):
            rows_here, docs_here, rows_prior, docs_prior, outs_here = inputs
            passed, attended, gradients = block_pass(rows_here, docs_here, rows_prior, docs_prior, outs_here, carried)
            return passed, (attended, gradients)

        start_carry = (jnp.zeros((slot_span, head_size), jnp.float32), jnp.zeros((slot_span, head_size), jnp.float32))
        _, results = lax.scan(advance, start_carry, (rows_all, docs_all, rows_before, docs_before, outs_all), reverse=True)
        return results

    attended_slots, grad_slots = lax.map(one_head, (proj_slots, doc_slots, out_slots))
    attended = attended_slots[routed_heads, seq_block, placed].astype(jnp.float32)
    head_outputs = (attended * gate_values[:, :, None]).astype(jnp.bfloat16)
    projection_grads = grad_slots[routed_heads, seq_block, placed]
    gate_grads = jnp.sum(cotangent.astype(jnp.float32) * attended, axis=2) * gate_values * (1.0 - gate_values)
    return head_outputs, projection_grads, gate_grads
```

```python
from functools import partial

import jax
import jax.numpy as jnp
from jax import lax
from jax.experimental import pallas as pl
from jax.experimental.pallas import tpu as pltpu
from jax.sharding import PartitionSpec as P

H = 64
CAP = 48
MASKED = -1e30
DOC_ROWS = 16
DOC_LANES = 64
PARTS = (6, 6, 4)
VMEM_LIMIT = 56 * 1024 * 1024

VMEM = pl.BlockSpec(memory_space=pltpu.VMEM)


def head_chunks(heads):
    total = sum(PARTS)
    edges = [0]
    for i in range(len(PARTS)):
        edges.append(round(heads * sum(PARTS[: i + 1]) / total))
    return [(a, b - a) for a, b in zip(edges[:-1], edges[1:]) if b > a]


def call(kernel, out_shape, *operands, aliases=None):
    return pl.pallas_call(
        kernel,
        out_shape=out_shape,
        in_specs=[VMEM] * len(operands),
        out_specs=jax.tree.map(lambda _: VMEM, out_shape),
        input_output_aliases=aliases or {},
        compiler_params=pltpu.CompilerParams(vmem_limit_bytes=VMEM_LIMIT),
    )(*operands)


def dot(a, b, dims):
    return lax.dot_general(a, b, (dims, ((), ())), preferred_element_type=jnp.float32)


NN = ((1,), (0,))
NT = ((1,), (1,))
TN = ((0,), (0,))


def dispatch_kernel(first, count, owned, flat_ref, doc_ref, proj_ref, out_grad_ref, *out_refs):
    me = lax.axis_index("head")
    rows = count * CAP
    routes = flat_ref.shape[1]
    width = proj_ref.shape[1]
    head_size = out_grad_ref.shape[1]
    flat = flat_ref[...]
    docs = doc_ref[...]
    lane = lax.broadcasted_iota(jnp.int32, (CAP, DOC_LANES), 1)
    for d, out_ref in enumerate(out_refs):
        base = ((me ^ d) * owned + first) * CAP
        hit = lax.broadcasted_iota(jnp.int32, (rows, routes), 0) == flat - base
        one_hot = jnp.where(hit, 1.0, 0.0).astype(jnp.bfloat16)
        out_ref[:rows, :width] = dot(one_hot, proj_ref[...], NN).astype(jnp.bfloat16)
        out_ref[:rows, width:] = dot(one_hot, out_grad_ref[...], NN).astype(jnp.bfloat16)
        slot_docs = jnp.sum(jnp.where(hit, docs, 0.0), axis=1, keepdims=True)
        table = jnp.zeros((CAP, DOC_LANES), jnp.float32)
        for h in range(count):
            table = jnp.where(lane == h, slot_docs[h * CAP : (h + 1) * CAP], table)
        thirds = [table[i * DOC_ROWS : (i + 1) * DOC_ROWS] for i in range(CAP // DOC_ROWS)]
        packed = jnp.concatenate(thirds + [jnp.zeros_like(thirds[0])], 1)
        blank = jnp.zeros((DOC_ROWS, head_size), jnp.float32)
        out_ref[rows:, :] = jnp.concatenate([blank, packed, blank], 1).astype(jnp.bfloat16)


def doc_table(packed):
    packed = packed.astype(jnp.float32)
    thirds = [packed[:, i * DOC_LANES : (i + 1) * DOC_LANES] for i in range(CAP // DOC_ROWS)]
    return jnp.concatenate(thirds, 0)


def attention_kernel(count, groups, *refs):
    blocks = refs[:groups]
    before_ref = refs[groups]
    near_ref, far_ref, own_ref, mask_ref = refs[groups + 1 :]
    me = lax.axis_index("head")
    rows = count * CAP
    head_size = blocks[0].shape[1] // 4
    scaling = head_size ** (-0.5)
    span = groups * CAP
    query_docs = jnp.concatenate(
        [doc_table(b[rows:, head_size : 3 * head_size]) for b in blocks], 0
    )
    before_docs = jnp.concatenate([doc_table(before_ref[d, rows:, :]) for d in range(groups)], 0)
    key_docs = jnp.concatenate([before_docs, query_docs], 0)
    key_docs = jnp.concatenate([key_docs, jnp.zeros_like(key_docs)], 1).T

    def order(index):
        return (me ^ (index // CAP)) * CAP + index % CAP

    row_order = order(lax.broadcasted_iota(jnp.int32, (span, 1), 0))
    column = lax.broadcasted_iota(jnp.int32, (1, 2 * span), 1)
    column_order = jnp.where(column < span, -1, order(jnp.maximum(column - span, 0)))
    mask_ref[...] = jnp.where(column_order <= row_order, 0.0, MASKED)

    for h in range(count):
        here = slice(h * CAP, (h + 1) * CAP)

        def piece(i):
            return jnp.concatenate([b[here, i * head_size : (i + 1) * head_size] for b in blocks], 0)

        def before(i):
            return jnp.concatenate(
                [before_ref[d, here, i * head_size : (i + 1) * head_size] for d in range(groups)], 0
            )

        queries = piece(0)
        key_rows = jnp.concatenate([before(0), piece(1)], 0)
        value_rows = jnp.concatenate([before(1), piece(2)], 0)
        grads_out = piece(3)
        scores = dot(queries, key_rows, NT) * scaling + mask_ref[...]
        scores = jnp.where(key_docs[h : h + 1, :] == query_docs[:, h : h + 1], scores, MASKED)
        row_max = jnp.max(scores, axis=1, keepdims=True)
        powers = jnp.exp(scores - row_max)
        row_sum = jnp.sum(powers, axis=1, keepdims=True)
        weights = powers * (1.0 / row_sum)
        weights_low = weights.astype(jnp.bfloat16)
        attended = dot(weights_low, value_rows, NN).astype(jnp.bfloat16)
        deltas = jnp.sum(
            grads_out.astype(jnp.float32) * attended.astype(jnp.float32), axis=1, keepdims=True
        )
        weight_grads = dot(grads_out, value_rows, NT)
        score_grads = (weights * (weight_grads - deltas)).astype(jnp.bfloat16)
        query_grads = (dot(score_grads, key_rows, NN) * scaling).astype(jnp.bfloat16)
        key_grads = dot(score_grads, queries, TN) * scaling
        value_grads = dot(weights_low, grads_out, TN)
        for d in range(groups):
            part = slice(d * CAP, (d + 1) * CAP)
            own = slice(span + d * CAP, span + (d + 1) * CAP)
            near_ref[d, here, :head_size] = attended[part]
            near_ref[d, here, head_size:] = query_grads[part]
            far_ref[d, here, :head_size] = key_grads[part].astype(jnp.bfloat16)
            far_ref[d, here, head_size:] = value_grads[part].astype(jnp.bfloat16)
            own_ref[d, here, :head_size] = key_grads[own]
            own_ref[d, here, head_size:] = value_grads[own]


def combine_kernel(groups, near_ref, own_ref, incoming_ref, *out_refs):
    half = near_ref.shape[2]
    for d in range(groups):
        out_refs[d][:, :half] = near_ref[d]
        total = own_ref[d] + incoming_ref[d].astype(jnp.float32)
        out_refs[d][:, half:] = total.astype(jnp.bfloat16)


def return_kernel(first, count, owned, groups, initial, *refs):
    flat_ref = refs[0]
    blocks = refs[1 : groups + 1]
    total_ref = None if initial else refs[groups + 1]
    out_ref = refs[-1]
    me = lax.axis_index("head")
    rows = count * CAP
    routes, lanes = flat_ref.shape
    tile = 256
    all_rows = jnp.concatenate([b[...] for b in blocks], 0)
    column = lax.broadcasted_iota(jnp.int32, (1, groups * rows), 1)
    slot = ((me ^ (column // rows)) * owned + first) * CAP + column % rows
    for start in range(0, routes, tile):
        part = slice(start, start + tile)
        hit = flat_ref[part, 0:1] == slot
        one_hot = jnp.where(hit, 1.0, 0.0).astype(jnp.bfloat16)
        taken = dot(one_hot, all_rows, NN)
        if not initial:
            taken = taken + total_ref[part, :].astype(jnp.float32)
        out_ref[part, :] = taken.astype(jnp.bfloat16)


def shifted(block, axis, distance):
    devices = range(lax.axis_size(axis))
    route = [(i, i + distance) for i in devices if i + distance in devices]
    return lax.ppermute(block, axis, route)


def exchanged(blocks):
    groups = len(blocks)
    return [blocks[0]] + [
        lax.ppermute(blocks[d], "head", [(i, i ^ d) for i in range(groups)])
        for d in range(1, groups)
    ]


def per_device(projections, routed_heads, slot_index, gate_logits, doc_lengths, cotangent):
    tokens, top, width = projections.shape
    head_size = width // 3
    routes = tokens * top
    groups = lax.axis_size("head")
    owned = H // groups
    bf16, f32 = jnp.bfloat16, jnp.float32

    offset = (lax.axis_index("seq") * groups + lax.axis_index("head")) * tokens
    positions = offset + jnp.arange(routes, dtype=jnp.int32) // top
    doc_ends = jnp.cumsum(doc_lengths)
    documents = jnp.sum((positions[None, :] >= doc_ends[:, None]).astype(f32), axis=0) + 1.0
    gate_values = jax.nn.sigmoid(gate_logits)
    grads_out = (cotangent.astype(f32) * gate_values[:, :, None]).astype(bf16)
    flat = (routed_heads * CAP + slot_index).reshape(routes)
    flat_columns = jnp.broadcast_to(flat[:, None], (routes, 128))
    rows_in = projections.reshape(routes, width)
    grads_in = grads_out.reshape(routes, head_size)

    chunks = head_chunks(owned)
    received = []
    for first, count in chunks:
        rows = count * CAP
        sent = call(
            partial(dispatch_kernel, first, count, owned),
            [jax.ShapeDtypeStruct((rows + DOC_ROWS, width + head_size), bf16)] * groups,
            flat[None, :],
            documents[None, :],
            rows_in,
            grads_in,
        )
        received.append(exchanged(sent))

    totals = None
    for (first, count), blocks in zip(chunks, received):
        rows = count * CAP
        before = shifted(jnp.stack([b[:, head_size : 3 * head_size] for b in blocks]), "seq", 1)
        pair = (groups, rows, 2 * head_size)
        near, far, own = pl.pallas_call(
            partial(attention_kernel, count, groups),
            out_shape=[
                jax.ShapeDtypeStruct(pair, bf16),
                jax.ShapeDtypeStruct(pair, bf16),
                jax.ShapeDtypeStruct(pair, f32),
            ],
            in_specs=[VMEM] * (groups + 1),
            out_specs=[VMEM] * 3,
            scratch_shapes=[pltpu.VMEM((groups * CAP, 2 * groups * CAP), f32)],
            compiler_params=pltpu.CompilerParams(vmem_limit_bytes=VMEM_LIMIT),
        )(*blocks, before)
        incoming = shifted(far, "seq", -1)
        home = call(
            partial(combine_kernel, groups),
            [jax.ShapeDtypeStruct((rows, 4 * head_size), bf16)] * groups,
            near,
            own,
            incoming,
        )
        home = exchanged(home)
        more = [] if totals is None else [totals]
        totals = call(
            partial(return_kernel, first, count, owned, groups, totals is None),
            jax.ShapeDtypeStruct((routes, 4 * head_size), bf16),
            flat_columns,
            *home,
            *more,
            aliases={groups + 1: 0} if more else None,
        )

    attended = totals[:, :head_size].reshape(tokens, top, head_size).astype(f32)
    projection_grads = totals[:, head_size:].reshape(tokens, top, width)
    head_outputs = (attended * gate_values[:, :, None]).astype(bf16)
    gate_grads = (
        jnp.sum(cotangent.astype(f32) * attended, axis=2) * gate_values * (1.0 - gate_values)
    )
    return (head_outputs, projection_grads, gate_grads)


def solution(mesh):
    return jax.shard_map(
        per_device,
        mesh=mesh,
        in_specs=(
            P(("seq", "head"), None, None),
            P(("seq", "head"), None),
            P(("seq", "head"), None),
            P(("seq", "head"), None),
            P(),
            P(("seq", "head"), None, None),
        ),
        out_specs=(
            P(("seq", "head"), None, None),
            P(("seq", "head"), None, None),
            P(("seq", "head"), None),
        ),
        check_vma=False,
    )
```

```python
from functools import partial

import jax
import jax.numpy as jnp
from jax import lax
from jax.experimental import pallas as pl
from jax.experimental.pallas import tpu as pltpu
from jax.sharding import PartitionSpec as P

H = 64
CAP = 48
MASKED = -1e30
DOC_ROWS = 16
DOC_LANES = 64
PARTS = (6, 6, 4)
KERNEL_BYTES = 20 * 1024 * 1024
TOGETHER = 2

VMEM = pl.BlockSpec(memory_space=pltpu.VMEM)


def head_chunks(heads):
    total = sum(PARTS)
    edges = [0]
    for i in range(len(PARTS)):
        edges.append(round(heads * sum(PARTS[: i + 1]) / total))
    return [(a, b - a) for a, b in zip(edges[:-1], edges[1:]) if b > a]


def call(kernel, out_shape, *operands, after=(), scratch=(), in_specs=None, pairs=0):
    waits = len(after)
    specs = in_specs or [VMEM] * len(operands)

    def body(*refs):
        kernel(*refs[waits:])

    return pl.pallas_call(
        body,
        out_shape=out_shape,
        in_specs=[pl.BlockSpec(memory_space=pl.ANY)] * waits + specs,
        out_specs=jax.tree.map(lambda _: VMEM, out_shape),
        scratch_shapes=list(scratch),
        cost_estimate=pl.CostEstimate(flops=6 * 10**9, bytes_accessed=20 * 10**6, transcendentals=0),
        compiler_params=pltpu.CompilerParams(vmem_limit_bytes=KERNEL_BYTES + 40 * pairs),
    )(*after, *operands)


def dot(a, b, dims):
    return lax.dot_general(a, b, (dims, ((), ())), preferred_element_type=jnp.float32)


NN = ((1,), (0,))
NT = ((1,), (1,))
TN = ((0,), (0,))


def one_hot(index, base, size, shape, dim):
    middle = size // 2
    near = jnp.clip(index - base, -1, size) - middle
    near = near.astype(jnp.float32).astype(jnp.bfloat16)
    spot = lax.broadcasted_iota(jnp.int32, tuple(n if i == dim else 1 for i, n in enumerate(shape)), dim)
    spot = (spot - middle).astype(jnp.float32).astype(jnp.bfloat16)
    one, zero = jnp.ones((), jnp.bfloat16), jnp.zeros((), jnp.bfloat16)
    return jnp.where(jnp.broadcast_to(near, shape) == jnp.broadcast_to(spot, shape), one, zero)


def spread(values):
    top, tokens = values.shape
    wide = jnp.broadcast_to(values.T[:, None, :], (tokens, top, top))
    return wide.reshape(tokens * top, top)


def own_route(routes, top):
    return lax.broadcasted_iota(jnp.int32, (routes, top), 1) == (
        lax.broadcasted_iota(jnp.int32, (routes, top), 0) % top
    )


def route_column(values):
    top, tokens = values.shape
    own = own_route(tokens * top, top)
    return jnp.sum(jnp.where(own, spread(values), 0.0), axis=1, keepdims=True)


def sigmoid(x):
    return 1.0 / (1.0 + jnp.exp(-x))


def prepare_kernel(heads_ref, slots_ref, logits_ref, doc_lengths_ref, proj_ref, cot_ref,
                   flat_ref, column_ref, docs_ref, rows_ref):
    top, tokens = heads_ref.shape
    routes = tokens * top
    width = proj_ref.shape[1]
    gate = route_column(sigmoid(logits_ref[...]))
    rows_ref[:, :width] = proj_ref[...]
    rows_ref[:, width:] = (cot_ref[...].astype(jnp.float32) * gate).astype(jnp.bfloat16)
    slots = route_column((heads_ref[...] * CAP + slots_ref[...]).astype(jnp.float32))
    slots = jnp.broadcast_to(slots, (routes, 128))
    column_ref[...] = slots.astype(jnp.int32)
    flat_ref[...] = slots.T[:8].astype(jnp.int32)
    place = lax.axis_index("seq") * lax.axis_size("head") + lax.axis_index("head")
    position = place * tokens + lax.broadcasted_iota(jnp.int32, docs_ref.shape, 1) // top
    docs = jnp.ones(docs_ref.shape, jnp.float32)
    end = 0
    for i in range(doc_lengths_ref.shape[0]):
        end = end + doc_lengths_ref[i]
        docs = docs + jnp.where(position >= end, 1.0, 0.0)
    docs_ref[...] = docs


def dispatch_kernel(first, count, owned, groups, flat_ref, docs_ref, rows_ref, *refs):
    out_refs = refs[:groups]
    hot_ref = refs[groups]
    me = lax.axis_index("head")
    rows = count * CAP
    routes, width = rows_ref.shape
    head_size = width // 4
    flat = flat_ref[0:1, :]
    docs = docs_ref[0:1, :].astype(jnp.bfloat16)
    lane = lax.broadcasted_iota(jnp.int32, (CAP, DOC_LANES), 1)
    for d, out_ref in enumerate(out_refs):
        base = ((me ^ d) * owned + first) * CAP
        hot = one_hot(flat, base, rows, (rows, routes), 0)
        hot_ref[d * rows : (d + 1) * rows, :] = hot
        marked = hot * docs
        slot_docs = marked[:, :128]
        for i in range(128, routes, 128):
            slot_docs = slot_docs + marked[:, i : i + 128]
        slot_docs = jnp.sum(slot_docs.astype(jnp.float32), axis=1, keepdims=True)
        table = jnp.zeros((CAP, DOC_LANES), jnp.float32)
        for h in range(count):
            table = jnp.where(lane == h, slot_docs[h * CAP : (h + 1) * CAP], table)
        thirds = [table[i * DOC_ROWS : (i + 1) * DOC_ROWS] for i in range(CAP // DOC_ROWS)]
        packed = jnp.concatenate(thirds + [jnp.zeros_like(thirds[0])], 1)
        blank = jnp.zeros((DOC_ROWS, head_size), jnp.float32)
        out_ref[rows:, :] = jnp.concatenate([blank, packed, blank], 1).astype(jnp.bfloat16)
    taken = dot(hot_ref[...], rows_ref[...], NN).astype(jnp.bfloat16)
    for d, out_ref in enumerate(out_refs):
        out_ref[:rows, :] = taken[d * rows : (d + 1) * rows]


def doc_table(packed):
    packed = packed.astype(jnp.float32)
    thirds = [packed[:, i * DOC_LANES : (i + 1) * DOC_LANES] for i in range(CAP // DOC_ROWS)]
    return jnp.concatenate(thirds, 0)


def attention_kernel(count, groups, *refs):
    blocks = refs[:groups]
    before_ref = refs[groups]
    near_ref, far_ref, own_ref, mask_ref = refs[groups + 1 :]
    me = lax.axis_index("head")
    rows = count * CAP
    head_size = blocks[0].shape[1] // 4
    scaling = head_size ** (-0.5)
    span = groups * CAP
    query_docs = jnp.concatenate(
        [doc_table(b[rows:, head_size : 3 * head_size]) for b in blocks], 0
    )
    before_docs = jnp.concatenate([doc_table(before_ref[d, rows:, :]) for d in range(groups)], 0)
    key_docs = jnp.concatenate([before_docs, query_docs], 0)
    key_docs = jnp.concatenate([key_docs, jnp.zeros_like(key_docs)], 1).T

    def order(index):
        return (me ^ (index // CAP)) * CAP + index % CAP

    row_order = order(lax.broadcasted_iota(jnp.int32, (span, 1), 0))
    column = lax.broadcasted_iota(jnp.int32, (1, 2 * span), 1)
    column_order = jnp.where(column < span, -1, order(jnp.maximum(column - span, 0)))
    mask_ref[...] = jnp.where(column_order <= row_order, 0.0, MASKED)

    def piece(h, i):
        here, part = slice(h * CAP, (h + 1) * CAP), slice(i * head_size, (i + 1) * head_size)
        return jnp.concatenate([b[here, part] for b in blocks], 0)

    def both(h, i):
        here, part = slice(h * CAP, (h + 1) * CAP), slice(i * head_size, (i + 1) * head_size)
        earlier = [before_ref[d, here, part] for d in range(groups)]
        return jnp.concatenate(earlier + [piece(h, i + 1)], 0)

    for start in range(0, count, TOGETHER):
        heads = range(start, min(start + TOGETHER, count))
        queries = [piece(h, 0) for h in heads]
        grads_out = [piece(h, 3) for h in heads]
        key_rows = [both(h, 0) for h in heads]
        value_rows = [both(h, 1) for h in heads]
        scores = [dot(q, k, NT) for q, k in zip(queries, key_rows)]
        weight_grads = [dot(g, v, NT) for g, v in zip(grads_out, value_rows)]
        weights = []
        for h, s in zip(heads, scores):
            s = s * scaling + mask_ref[...]
            s = jnp.where(key_docs[h : h + 1, :] == query_docs[:, h : h + 1], s, MASKED)
            powers = jnp.exp(s - jnp.max(s, axis=1, keepdims=True))
            weights.append(powers * (1.0 / jnp.sum(powers, axis=1, keepdims=True)))
        weights_low = [w.astype(jnp.bfloat16) for w in weights]
        attended = [dot(w, v, NN).astype(jnp.bfloat16) for w, v in zip(weights_low, value_rows)]
        value_grads = [dot(w, g, TN) for w, g in zip(weights_low, grads_out)]
        deltas = [
            jnp.sum(g.astype(jnp.float32) * a.astype(jnp.float32), axis=1, keepdims=True)
            for g, a in zip(grads_out, attended)
        ]
        score_grads = [
            (w * (wg - d)).astype(jnp.bfloat16) for w, wg, d in zip(weights, weight_grads, deltas)
        ]
        query_grads = [
            (dot(s, k, NN) * scaling).astype(jnp.bfloat16) for s, k in zip(score_grads, key_rows)
        ]
        key_grads = [dot(s, q, TN) * scaling for s, q in zip(score_grads, queries)]
        for i, h in enumerate(heads):
            here = slice(h * CAP, (h + 1) * CAP)
            for d in range(groups):
                part = slice(d * CAP, (d + 1) * CAP)
                own = slice(span + d * CAP, span + (d + 1) * CAP)
                near_ref[d, here, :head_size] = attended[i][part]
                near_ref[d, here, head_size:] = query_grads[i][part]
                far_ref[d, here, :head_size] = key_grads[i][part].astype(jnp.bfloat16)
                far_ref[d, here, head_size:] = value_grads[i][part].astype(jnp.bfloat16)
                own_ref[d, here, :head_size] = key_grads[i][own]
                own_ref[d, here, head_size:] = value_grads[i][own]


def combine_kernel(groups, near_ref, own_ref, incoming_ref, *out_refs):
    half = near_ref.shape[2]
    for d in range(groups):
        out_refs[d][:, :half] = near_ref[d]
        total = own_ref[d] + incoming_ref[d].astype(jnp.float32)
        out_refs[d][:, half:] = total.astype(jnp.bfloat16)


def routed(first, count, owned, groups, refs):
    column_ref = refs[0]
    blocks = refs[1 : groups + 1]
    hot_ref = refs[-1]
    me = lax.axis_index("head")
    rows = count * CAP
    routes = column_ref.shape[0]
    for d in range(groups):
        base = ((me ^ d) * owned + first) * CAP
        hot = one_hot(column_ref[:, 0:1], base, rows, (routes, rows), 1)
        hot_ref[:, d * rows : (d + 1) * rows] = hot
    return dot(hot_ref[...], jnp.concatenate([b[...] for b in blocks], 0), NN)


def return_kernel(first, count, owned, groups, initial, *refs):
    taken = routed(first, count, owned, groups, refs)
    if not initial:
        taken = taken + refs[groups + 1][...].astype(jnp.float32)
    refs[-2][...] = taken.astype(jnp.bfloat16)


def finish_kernel(first, count, owned, groups, initial, *refs):
    logits_ref, cot_ref, heads_out_ref, proj_grads_ref, gate_grads_ref = refs[-6:-1]
    taken = routed(first, count, owned, groups, refs)
    if not initial:
        taken = taken + refs[groups + 1][...].astype(jnp.float32)
    head_size = cot_ref.shape[1]
    top, tokens = logits_ref.shape
    routes = tokens * top
    proj_grads_ref[...] = taken[:, head_size:].astype(jnp.bfloat16)
    attended = taken[:, :head_size]
    gate_table = sigmoid(logits_ref[...])
    heads_out_ref[...] = (attended * route_column(gate_table)).astype(jnp.bfloat16)
    sums = jnp.sum(cot_ref[...].astype(jnp.float32) * attended, axis=1, keepdims=True)
    sums = jnp.where(own_route(routes, top), sums, 0.0).reshape(tokens, top, top)
    gate_grads_ref[...] = jnp.sum(sums, axis=1).T * gate_table * (1.0 - gate_table)


def shifted(block, axis, distance):
    devices = range(lax.axis_size(axis))
    route = [(i, i + distance) for i in devices if i + distance in devices]
    return lax.ppermute(block, axis, route)


def exchanged(blocks):
    groups = len(blocks)
    return [blocks[0]] + [
        lax.ppermute(blocks[d], "head", [(i, i ^ d) for i in range(groups)])
        for d in range(1, groups)
    ]


def per_device(projections, routed_heads, slot_index, gate_logits, doc_lengths, cotangent):
    tokens, top, width = projections.shape
    head_size = width // 3
    routes = tokens * top
    groups = lax.axis_size("head")
    owned = H // groups
    bf16, f32 = jnp.bfloat16, jnp.float32

    shape = jax.ShapeDtypeStruct
    logits = gate_logits.T
    cot_rows = cotangent.reshape(routes, head_size)
    flat, columns, documents, rows_in = call(
        prepare_kernel,
        [
            shape((8, routes), jnp.int32),
            shape((routes, 128), jnp.int32),
            shape((8, routes), f32),
            shape((routes, width + head_size), bf16),
        ],
        routed_heads.T,
        slot_index.T,
        logits,
        doc_lengths,
        projections.reshape(routes, width),
        cot_rows,
        in_specs=[VMEM] * 3 + [pl.BlockSpec(memory_space=pltpu.SMEM)] + [VMEM] * 2,
    )

    chunks = head_chunks(owned)
    last = len(chunks) - 1
    blocks_out = []
    for first, count in chunks:
        rows = count * CAP
        sent = call(
            partial(dispatch_kernel, first, count, owned, groups),
            [shape((rows + DOC_ROWS, width + head_size), bf16)] * groups,
            flat,
            documents,
            rows_in,
            scratch=[pltpu.VMEM((groups * rows, routes), bf16)],
        )
        blocks_out.append(sent)
    received = [exchanged(sent) for sent in blocks_out]

    homes, fars = [], []
    for i, ((first, count), blocks) in enumerate(zip(chunks, received)):
        rows = count * CAP
        if i > 0:
            *blocks, fars[-1] = lax.optimization_barrier((*blocks, fars[-1]))
        else:
            waits = [sent[0] for sent in blocks_out[1:]]
            blocks = lax.optimization_barrier((*blocks, *waits))[: len(blocks)]
        before = shifted(jnp.stack([b[:, head_size : 3 * head_size] for b in blocks]), "seq", 1)
        if i > 0:
            homes.append(finish_chunk(fars[-1]))
        pair = (groups, rows, 2 * head_size)
        near, far, own = call(
            partial(attention_kernel, count, groups),
            [shape(pair, bf16), shape(pair, bf16), shape(pair, f32)],
            *blocks,
            before,
            after=homes[-1][:1] if homes else (),
            scratch=[pltpu.VMEM((groups * CAP, 2 * groups * CAP), f32)],
            pairs=2 * (groups * CAP) ** 2,
        )
        fars.append(far)

        def finish_chunk(far, near=near, own=own, rows=rows):
            return call(
                partial(combine_kernel, groups),
                [shape((rows, 4 * head_size), bf16)] * groups,
                near,
                own,
                shifted(far, "seq", -1),
            )

    homes.append(finish_chunk(fars[-1]))
    total = []
    for i, ((first, count), home) in enumerate(zip(chunks, homes)):
        rows = count * CAP
        operands = [columns, *exchanged(home), *total]
        scratch = [pltpu.VMEM((routes, groups * rows), bf16)]
        if i < last:
            total = [
                call(
                    partial(return_kernel, first, count, owned, groups, i == 0),
                    shape((routes, 4 * head_size), bf16),
                    *operands,
                    after=[homes[i + 1][0]],
                    scratch=scratch,
                )
            ]
    head_outputs, projection_grads, gate_grads = call(
        partial(finish_kernel, first, count, owned, groups, last == 0),
        [
            shape((routes, head_size), bf16),
            shape((routes, width), bf16),
            shape(logits.shape, f32),
        ],
        *operands,
        logits,
        cot_rows,
        scratch=scratch,
    )
    return (
        head_outputs.reshape(tokens, top, head_size),
        projection_grads.reshape(tokens, top, width),
        gate_grads.T,
    )


def solution(mesh):
    return jax.shard_map(
        per_device,
        mesh=mesh,
        in_specs=(
            P(("seq", "head"), None, None),
            P(("seq", "head"), None),
            P(("seq", "head"), None),
            P(("seq", "head"), None),
            P(),
            P(("seq", "head"), None, None),
        ),
        out_specs=(
            P(("seq", "head"), None, None),
            P(("seq", "head"), None, None),
            P(("seq", "head"), None),
        ),
        check_vma=False,
    )
```

```python
from functools import partial

import jax
import jax.numpy as jnp
from jax import lax
from jax.experimental import pallas as pl
from jax.experimental.pallas import tpu as pltpu
from jax.sharding import PartitionSpec as P

H = 64
CAP = 48
MASKED = -1e30
DOC_ROWS = 16
DOC_LANES = 64
PARTS = (6, 6, 4)
COSTS = (6, 6, 6, 6)
PREPARE_BYTES = 60 * 1024 * 1024
KERNEL_BYTES = 20 * 1024 * 1024
TOGETHER = 2

VMEM = pl.BlockSpec(memory_space=pltpu.VMEM)
ANY = pl.BlockSpec(memory_space=pl.ANY)
HBM = pl.BlockSpec(memory_space=pltpu.HBM)


def head_chunks(heads):
    total = sum(PARTS)
    edges = [0]
    for i in range(len(PARTS)):
        edges.append(round(heads * sum(PARTS[: i + 1]) / total))
    return [(a, b - a) for a, b in zip(edges[:-1], edges[1:]) if b > a]


def call(kernel, out_shape, *operands, after=(), scratch=(), in_specs=None, pairs=0, cost=0.0, limit=0):
    waits = len(after)
    specs = in_specs or [VMEM] * len(operands)

    def body(*refs):
        kernel(*refs[waits:])

    return pl.pallas_call(
        body,
        out_shape=out_shape,
        in_specs=[ANY] * waits + specs,
        out_specs=jax.tree.map(lambda _: VMEM, out_shape),
        scratch_shapes=list(scratch),
        cost_estimate=pl.CostEstimate(
            flops=int(cost * 1e9), bytes_accessed=int(cost * 3.4e6), transcendentals=0
        ),
        compiler_params=pltpu.CompilerParams(vmem_limit_bytes=limit or KERNEL_BYTES + 40 * pairs),
    )(*after, *operands)


def dot(a, b, dims):
    return lax.dot_general(a, b, (dims, ((), ())), preferred_element_type=jnp.float32)


NN = ((1,), (0,))
NT = ((1,), (1,))
TN = ((0,), (0,))


def one_hot(index, base, size, shape, dim):
    middle = size // 2
    near = jnp.clip(index - base, -1, size) - middle
    near = near.astype(jnp.float32).astype(jnp.bfloat16)
    spot = lax.broadcasted_iota(jnp.int32, tuple(n if i == dim else 1 for i, n in enumerate(shape)), dim)
    spot = (spot - middle).astype(jnp.float32).astype(jnp.bfloat16)
    one, zero = jnp.ones((), jnp.bfloat16), jnp.zeros((), jnp.bfloat16)
    return jnp.where(jnp.broadcast_to(near, shape) == jnp.broadcast_to(spot, shape), one, zero)


def spread(values):
    top, tokens = values.shape
    wide = jnp.broadcast_to(values.T[:, None, :], (tokens, top, top))
    return wide.reshape(tokens * top, top)


def own_route(routes, top):
    return lax.broadcasted_iota(jnp.int32, (routes, top), 1) == (
        lax.broadcasted_iota(jnp.int32, (routes, top), 0) % top
    )


def route_column(values):
    top, tokens = values.shape
    own = own_route(tokens * top, top)
    return jnp.sum(jnp.where(own, spread(values), 0.0), axis=1, keepdims=True)


def sigmoid(x):
    return 1.0 / (1.0 + jnp.exp(-x))


def prepare_kernel(first, count, owned, groups, heads_in, slots_in, logits_in, doc_lengths_ref,
                   proj_in, cot_in, *refs):
    flat_ref, column_ref, docs_ref, rows_ref = refs[:4]
    out_refs = refs[4 : groups + 4]
    heads_ref, slots_ref, logits_ref, proj_ref, cot_ref, hot_ref, sems = refs[groups + 4 :]
    pairs = [
        (heads_in, heads_ref), (slots_in, slots_ref), (logits_in, logits_ref),
        (cot_in, cot_ref), (proj_in, proj_ref),
    ]
    copies = [pltpu.make_async_copy(a, b, sems.at[i]) for i, (a, b) in enumerate(pairs)]
    for copy in copies:
        copy.start()
    for copy in copies[:3]:
        copy.wait()
    top, tokens = heads_ref.shape
    routes = tokens * top
    width = proj_ref.shape[1]
    gate = route_column(sigmoid(logits_ref[...]))
    slots = route_column((heads_ref[...] * CAP + slots_ref[...]).astype(jnp.float32))
    slots = jnp.broadcast_to(slots, (routes, 128))
    column_ref[...] = slots.astype(jnp.int32)
    flat_ref[...] = slots.T[:8].astype(jnp.int32)
    place = lax.axis_index("seq") * lax.axis_size("head") + lax.axis_index("head")
    position = place * tokens + lax.broadcasted_iota(jnp.int32, docs_ref.shape, 1) // top
    docs = jnp.ones(docs_ref.shape, jnp.float32)
    end = 0
    for i in range(doc_lengths_ref.shape[0]):
        end = end + doc_lengths_ref[i]
        docs = docs + jnp.where(position >= end, 1.0, 0.0)
    docs_ref[...] = docs
    copies[3].wait()
    rows_ref[:, width:] = (cot_ref[...].astype(jnp.float32) * gate).astype(jnp.bfloat16)
    copies[4].wait()
    rows_ref[:, :width] = proj_ref[...]
    dispatch_kernel(first, count, owned, groups, flat_ref, docs_ref, rows_ref, *out_refs, hot_ref)


def dispatch_kernel(first, count, owned, groups, flat_ref, docs_ref, rows_ref, *refs):
    out_refs = refs[:groups]
    hot_ref = refs[groups]
    me = lax.axis_index("head")
    rows = count * CAP
    routes, width = rows_ref.shape
    head_size = width // 4
    flat = flat_ref[0:1, :]
    docs = docs_ref[0:1, :].astype(jnp.bfloat16)
    lane = lax.broadcasted_iota(jnp.int32, (CAP, DOC_LANES), 1)
    for d, out_ref in enumerate(out_refs):
        base = ((me ^ d) * owned + first) * CAP
        hot = one_hot(flat, base, rows, (rows, routes), 0)
        hot_ref[d * rows : (d + 1) * rows, :] = hot
        marked = hot * docs
        slot_docs = marked[:, :128]
        for i in range(128, routes, 128):
            slot_docs = slot_docs + marked[:, i : i + 128]
        slot_docs = jnp.sum(slot_docs.astype(jnp.float32), axis=1, keepdims=True)
        table = jnp.zeros((CAP, DOC_LANES), jnp.float32)
        for h in range(count):
            table = jnp.where(lane == h, slot_docs[h * CAP : (h + 1) * CAP], table)
        thirds = [table[i * DOC_ROWS : (i + 1) * DOC_ROWS] for i in range(CAP // DOC_ROWS)]
        packed = jnp.concatenate(thirds + [jnp.zeros_like(thirds[0])], 1)
        blank = jnp.zeros((DOC_ROWS, head_size), jnp.float32)
        out_ref[rows:, :] = jnp.concatenate([blank, packed, blank], 1).astype(jnp.bfloat16)
    taken = dot(hot_ref[...], rows_ref[...], NN).astype(jnp.bfloat16)
    for d, out_ref in enumerate(out_refs):
        out_ref[:rows, :] = taken[d * rows : (d + 1) * rows]


def doc_table(packed):
    packed = packed.astype(jnp.float32)
    thirds = [packed[:, i * DOC_LANES : (i + 1) * DOC_LANES] for i in range(CAP // DOC_ROWS)]
    return jnp.concatenate(thirds, 0)


def attention_kernel(count, groups, *refs):
    blocks = refs[:groups]
    before_ref = refs[groups]
    near_ref, far_ref, own_ref, mask_ref = refs[groups + 1 :]
    me = lax.axis_index("head")
    rows = count * CAP
    head_size = blocks[0].shape[1] // 4
    scaling = head_size ** (-0.5)
    span = groups * CAP
    query_docs = jnp.concatenate(
        [doc_table(b[rows:, head_size : 3 * head_size]) for b in blocks], 0
    )
    before_docs = jnp.concatenate([doc_table(before_ref[d, rows:, :]) for d in range(groups)], 0)
    key_docs = jnp.concatenate([before_docs, query_docs], 0)
    key_docs = jnp.concatenate([key_docs, jnp.zeros_like(key_docs)], 1).T

    def order(index):
        return (me ^ (index // CAP)) * CAP + index % CAP

    row_order = order(lax.broadcasted_iota(jnp.int32, (span, 1), 0))
    column = lax.broadcasted_iota(jnp.int32, (1, 2 * span), 1)
    column_order = jnp.where(column < span, -1, order(jnp.maximum(column - span, 0)))
    mask_ref[...] = jnp.where(column_order <= row_order, 0.0, MASKED)

    def piece(h, i):
        here, part = slice(h * CAP, (h + 1) * CAP), slice(i * head_size, (i + 1) * head_size)
        return jnp.concatenate([b[here, part] for b in blocks], 0)

    def both(h, i):
        here, part = slice(h * CAP, (h + 1) * CAP), slice(i * head_size, (i + 1) * head_size)
        earlier = [before_ref[d, here, part] for d in range(groups)]
        return jnp.concatenate(earlier + [piece(h, i + 1)], 0)

    for start in range(0, count, TOGETHER):
        heads = range(start, min(start + TOGETHER, count))
        queries = [piece(h, 0) for h in heads]
        grads_out = [piece(h, 3) for h in heads]
        key_rows = [both(h, 0) for h in heads]
        value_rows = [both(h, 1) for h in heads]
        scores = [dot(q, k, NT) for q, k in zip(queries, key_rows)]
        weight_grads = [dot(g, v, NT) for g, v in zip(grads_out, value_rows)]
        weights = []
        for h, s in zip(heads, scores):
            s = s * scaling + mask_ref[...]
            s = jnp.where(key_docs[h : h + 1, :] == query_docs[:, h : h + 1], s, MASKED)
            powers = jnp.exp(s - jnp.max(s, axis=1, keepdims=True))
            weights.append(powers * (1.0 / jnp.sum(powers, axis=1, keepdims=True)))
        weights_low = [w.astype(jnp.bfloat16) for w in weights]
        attended = [dot(w, v, NN).astype(jnp.bfloat16) for w, v in zip(weights_low, value_rows)]
        value_grads = [dot(w, g, TN) for w, g in zip(weights_low, grads_out)]
        deltas = [
            jnp.sum(g.astype(jnp.float32) * a.astype(jnp.float32), axis=1, keepdims=True)
            for g, a in zip(grads_out, attended)
        ]
        score_grads = [
            (w * (wg - d)).astype(jnp.bfloat16) for w, wg, d in zip(weights, weight_grads, deltas)
        ]
        query_grads = [
            (dot(s, k, NN) * scaling).astype(jnp.bfloat16) for s, k in zip(score_grads, key_rows)
        ]
        key_grads = [dot(s, q, TN) * scaling for s, q in zip(score_grads, queries)]
        for i, h in enumerate(heads):
            here = slice(h * CAP, (h + 1) * CAP)
            for d in range(groups):
                part = slice(d * CAP, (d + 1) * CAP)
                own = slice(span + d * CAP, span + (d + 1) * CAP)
                near_ref[d, here, :head_size] = attended[i][part]
                near_ref[d, here, head_size:] = query_grads[i][part]
                far_ref[d, here, :head_size] = key_grads[i][part].astype(jnp.bfloat16)
                far_ref[d, here, head_size:] = value_grads[i][part].astype(jnp.bfloat16)
                own_ref[d, here, :head_size] = key_grads[i][own]
                own_ref[d, here, head_size:] = value_grads[i][own]


def combine_kernel(groups, near_ref, own_ref, incoming_ref, *out_refs):
    half = near_ref.shape[2]
    for d in range(groups):
        out_refs[d][:, :half] = near_ref[d]
        total = own_ref[d] + incoming_ref[d].astype(jnp.float32)
        out_refs[d][:, half:] = total.astype(jnp.bfloat16)


def routed(first, count, owned, groups, refs):
    column_ref = refs[0]
    blocks = refs[1 : groups + 1]
    hot_ref = refs[-1]
    me = lax.axis_index("head")
    rows = count * CAP
    routes = column_ref.shape[0]
    for d in range(groups):
        base = ((me ^ d) * owned + first) * CAP
        hot = one_hot(column_ref[:, 0:1], base, rows, (routes, rows), 1)
        hot_ref[:, d * rows : (d + 1) * rows] = hot
    return dot(hot_ref[...], jnp.concatenate([b[...] for b in blocks], 0), NN)


def return_kernel(first, count, owned, groups, initial, *refs):
    taken = routed(first, count, owned, groups, refs)
    if not initial:
        taken = taken + refs[groups + 1][...].astype(jnp.float32)
    refs[-2][...] = taken.astype(jnp.bfloat16)


def finish_kernel(first, count, owned, groups, initial, *refs):
    logits_ref, cot_ref, heads_out_ref, proj_grads_ref, gate_grads_ref = refs[-6:-1]
    taken = routed(first, count, owned, groups, refs)
    if not initial:
        taken = taken + refs[groups + 1][...].astype(jnp.float32)
    head_size = cot_ref.shape[1]
    top, tokens = logits_ref.shape
    routes = tokens * top
    proj_grads_ref[...] = taken[:, head_size:].astype(jnp.bfloat16)
    attended = taken[:, :head_size]
    gate_table = sigmoid(logits_ref[...])
    heads_out_ref[...] = (attended * route_column(gate_table)).astype(jnp.bfloat16)
    sums = jnp.sum(cot_ref[...].astype(jnp.float32) * attended, axis=1, keepdims=True)
    sums = jnp.where(own_route(routes, top), sums, 0.0).reshape(tokens, top, top)
    gate_grads_ref[...] = jnp.sum(sums, axis=1).T * gate_table * (1.0 - gate_table)


def shifted(block, axis, distance):
    devices = range(lax.axis_size(axis))
    route = [(i, i + distance) for i in devices if i + distance in devices]
    return lax.ppermute(block, axis, route)


def exchanged(blocks):
    groups = len(blocks)
    return [blocks[0]] + [
        lax.ppermute(blocks[d], "head", [(i, i ^ d) for i in range(groups)])
        for d in range(1, groups)
    ]


def per_device(projections, routed_heads, slot_index, gate_logits, doc_lengths, cotangent):
    tokens, top, width = projections.shape
    head_size = width // 3
    routes = tokens * top
    groups = lax.axis_size("head")
    owned = H // groups
    bf16, f32 = jnp.bfloat16, jnp.float32

    shape = jax.ShapeDtypeStruct
    logits = gate_logits.T
    cot_rows = cotangent.reshape(routes, head_size)
    chunks = head_chunks(owned)
    last = len(chunks) - 1

    def sent_shapes(count):
        return [shape((count * CAP + DOC_ROWS, width + head_size), bf16)] * groups

    def hot_scratch(count):
        return pltpu.VMEM((groups * count * CAP, routes), bf16)

    flat, columns, documents, rows_in, *sent = call(
        partial(prepare_kernel, *chunks[0], owned, groups),
        [
            shape((8, routes), jnp.int32),
            shape((routes, 128), jnp.int32),
            shape((8, routes), f32),
            shape((routes, width + head_size), bf16),
        ]
        + sent_shapes(chunks[0][1]),
        routed_heads.T,
        slot_index.T,
        logits,
        doc_lengths,
        projections.reshape(routes, width),
        cot_rows,
        in_specs=[ANY] * 3 + [pl.BlockSpec(memory_space=pltpu.SMEM)] + [ANY] * 2,
        scratch=[
            pltpu.VMEM((top, tokens), jnp.int32),
            pltpu.VMEM((top, tokens), jnp.int32),
            pltpu.VMEM((top, tokens), f32),
            pltpu.VMEM((routes, width), bf16),
            pltpu.VMEM((routes, head_size), bf16),
            hot_scratch(chunks[0][1]),
            pltpu.SemaphoreType.DMA((5,)),
        ],
        limit=PREPARE_BYTES,
        cost=COSTS[0],
    )
    blocks_out = [sent]
    for first, count in chunks[1:]:
        sent = call(
            partial(dispatch_kernel, first, count, owned, groups),
            sent_shapes(count),
            flat,
            documents,
            rows_in,
            scratch=[hot_scratch(count)],
            cost=COSTS[0],
        )
        blocks_out.append(sent)
    received = []
    for i, sent in enumerate(blocks_out):
        with jax.named_scope(f"send_out_{i}"):
            received.append(exchanged(sent))

    homes, fars, returned = [], [], []
    for i, ((first, count), blocks) in enumerate(zip(chunks, received)):
        rows = count * CAP
        if i > 0:
            *blocks, _ = lax.optimization_barrier((*blocks, fars[-1]))
        else:
            waits = [sent[0] for sent in blocks_out[1:]]
            blocks = lax.optimization_barrier((*blocks, *waits))[: len(blocks)]
        with jax.named_scope(f"send_next_{i}"):
            before = shifted(jnp.stack([b[:, head_size : 3 * head_size] for b in blocks]), "seq", 1)
        if i > 0:
            homes.append(finish_chunk(incoming))
            with jax.named_scope(f"send_home_{i - 1}"):
                returned.append(exchanged(homes[-1]))
        pair = (groups, rows, 2 * head_size)
        near, far, own = call(
            partial(attention_kernel, count, groups),
            [shape(pair, bf16), shape(pair, bf16), shape(pair, f32)],
            *blocks,
            before,
            after=[homes[-1][0]] if homes else (),
            scratch=[pltpu.VMEM((groups * CAP, 2 * groups * CAP), f32)],
            pairs=2 * (groups * CAP) ** 2,
            cost=COSTS[1],
        )
        fars.append(far)

        with jax.named_scope(f"send_back_{i}"):
            incoming = shifted(far, "seq", -1)

        def finish_chunk(incoming, near=near, own=own, rows=rows):
            return call(
                partial(combine_kernel, groups),
                [shape((rows, 4 * head_size), bf16)] * groups,
                near,
                own,
                incoming,
                cost=COSTS[2],
            )

    homes.append(finish_chunk(incoming))
    with jax.named_scope(f"send_home_{last}"):
        returned.append(exchanged(homes[-1]))
    total = []
    for i, ((first, count), home) in enumerate(zip(chunks, homes)):
        rows = count * CAP
        operands = [columns, *returned[i], *total]
        scratch = [pltpu.VMEM((routes, groups * rows), bf16)]
        if i < last:
            total = [
                call(
                    partial(return_kernel, first, count, owned, groups, i == 0),
                    shape((routes, 4 * head_size), bf16),
                    *operands,
                    after=[homes[i + 1][0]],
                    scratch=scratch,
                    cost=COSTS[3],
                )
            ]
    head_outputs, projection_grads, gate_grads = call(
        partial(finish_kernel, first, count, owned, groups, last == 0),
        [
            shape((routes, head_size), bf16),
            shape((routes, width), bf16),
            shape(logits.shape, f32),
        ],
        *operands,
        logits,
        cot_rows,
        scratch=scratch,
    )
    return (
        head_outputs.reshape(tokens, top, head_size),
        projection_grads.reshape(tokens, top, width),
        gate_grads.T,
    )


def solution(mesh):
    return jax.shard_map(
        per_device,
        mesh=mesh,
        in_specs=(
            P(("seq", "head"), None, None),
            P(("seq", "head"), None),
            P(("seq", "head"), None),
            P(("seq", "head"), None),
            P(),
            P(("seq", "head"), None, None),
        ),
        out_specs=(
            P(("seq", "head"), None, None),
            P(("seq", "head"), None, None),
            P(("seq", "head"), None),
        ),
        check_vma=False,
    )
```

```python
from functools import partial

import jax
import jax.numpy as jnp
from jax import lax
from jax.experimental import pallas as pl
from jax.experimental.pallas import tpu as pltpu
from jax.sharding import PartitionSpec as P

H = 64
CAP = 48
MASKED = -1e30
DOC_ROWS = 16
DOC_LANES = 64
PARTS = (6, 6, 4)
COSTS = (6, 6, 6, 6)
PREPARE_BYTES = 60 * 1024 * 1024
KERNEL_BYTES = 20 * 1024 * 1024
TOGETHER = 6

VMEM = pl.BlockSpec(memory_space=pltpu.VMEM)
ANY = pl.BlockSpec(memory_space=pl.ANY)
HBM = pl.BlockSpec(memory_space=pltpu.HBM)


def head_chunks(heads):
    total = sum(PARTS)
    edges = [0]
    for i in range(len(PARTS)):
        edges.append(round(heads * sum(PARTS[: i + 1]) / total))
    return [(a, b - a) for a, b in zip(edges[:-1], edges[1:]) if b > a]


def call(kernel, out_shape, *operands, after=(), scratch=(), in_specs=None, pairs=0, cost=0.0, limit=0):
    waits = len(after)
    specs = in_specs or [VMEM] * len(operands)

    def body(*refs):
        kernel(*refs[waits:])

    return pl.pallas_call(
        body,
        out_shape=out_shape,
        in_specs=[ANY] * waits + specs,
        out_specs=jax.tree.map(lambda _: VMEM, out_shape),
        scratch_shapes=list(scratch),
        cost_estimate=pl.CostEstimate(
            flops=int(cost * 1e9), bytes_accessed=int(cost * 3.4e6), transcendentals=0
        ),
        compiler_params=pltpu.CompilerParams(vmem_limit_bytes=limit or KERNEL_BYTES + 40 * pairs),
    )(*after, *operands)


def dot(a, b, dims):
    return lax.dot_general(a, b, (dims, ((), ())), preferred_element_type=jnp.float32)


NN = ((1,), (0,))
NT = ((1,), (1,))
TN = ((0,), (0,))


def one_hot(index, base, size, shape, dim):
    middle = size // 2
    near = jnp.clip(index - base, -1, size) - middle
    near = near.astype(jnp.float32).astype(jnp.bfloat16)
    spot = lax.broadcasted_iota(jnp.int32, tuple(n if i == dim else 1 for i, n in enumerate(shape)), dim)
    spot = (spot - middle).astype(jnp.float32).astype(jnp.bfloat16)
    one, zero = jnp.ones((), jnp.bfloat16), jnp.zeros((), jnp.bfloat16)
    return jnp.where(jnp.broadcast_to(near, shape) == jnp.broadcast_to(spot, shape), one, zero)


def spread(values):
    top, tokens = values.shape
    wide = jnp.broadcast_to(values.T[:, None, :], (tokens, top, top))
    return wide.reshape(tokens * top, top)


def own_route(routes, top):
    return lax.broadcasted_iota(jnp.int32, (routes, top), 1) == (
        lax.broadcasted_iota(jnp.int32, (routes, top), 0) % top
    )


def route_column(values):
    top, tokens = values.shape
    own = own_route(tokens * top, top)
    return jnp.sum(jnp.where(own, spread(values), 0.0), axis=1, keepdims=True)


def sigmoid(x):
    return 1.0 / (1.0 + jnp.exp(-x))


def prepare_kernel(first, count, owned, groups, heads_in, slots_in, logits_in, doc_lengths_ref,
                   proj_in, cot_in, *refs):
    flat_ref, column_ref, docs_ref, rows_ref = refs[:4]
    out_refs = refs[4 : groups + 4]
    heads_ref, slots_ref, logits_ref, proj_ref, cot_ref, hot_ref, sems = refs[groups + 4 :]
    pairs = [
        (heads_in, heads_ref), (slots_in, slots_ref), (logits_in, logits_ref),
        (cot_in, cot_ref), (proj_in, proj_ref),
    ]
    copies = [pltpu.make_async_copy(a, b, sems.at[i]) for i, (a, b) in enumerate(pairs)]
    for copy in copies:
        copy.start()
    for copy in copies[:3]:
        copy.wait()
    top, tokens = heads_ref.shape
    routes = tokens * top
    width = proj_ref.shape[1]
    gate = route_column(sigmoid(logits_ref[...]))
    slots = route_column((heads_ref[...] * CAP + slots_ref[...]).astype(jnp.float32))
    slots = jnp.broadcast_to(slots, (routes, 128))
    column_ref[...] = slots.astype(jnp.int32)
    flat_ref[...] = slots.T[:8].astype(jnp.int32)
    place = lax.axis_index("seq") * lax.axis_size("head") + lax.axis_index("head")
    position = place * tokens + lax.broadcasted_iota(jnp.int32, docs_ref.shape, 1) // top
    docs = jnp.ones(docs_ref.shape, jnp.float32)
    end = 0
    for i in range(doc_lengths_ref.shape[0]):
        end = end + doc_lengths_ref[i]
        docs = docs + jnp.where(position >= end, 1.0, 0.0)
    docs_ref[...] = docs
    copies[3].wait()
    rows_ref[:, width:] = (cot_ref[...].astype(jnp.float32) * gate).astype(jnp.bfloat16)
    copies[4].wait()
    rows_ref[:, :width] = proj_ref[...]
    dispatch_kernel(first, count, owned, groups, flat_ref, docs_ref, rows_ref, *out_refs, hot_ref)


def dispatch_kernel(first, count, owned, groups, flat_ref, docs_ref, rows_ref, *refs):
    out_refs = refs[:groups]
    hot_ref = refs[groups]
    me = lax.axis_index("head")
    rows = count * CAP
    routes, width = rows_ref.shape
    head_size = width // 4
    flat = flat_ref[0:1, :]
    docs = docs_ref[0:1, :].astype(jnp.bfloat16)
    lane = lax.broadcasted_iota(jnp.int32, (CAP, DOC_LANES), 1)
    for d, out_ref in enumerate(out_refs):
        base = ((me ^ d) * owned + first) * CAP
        hot = one_hot(flat, base, rows, (rows, routes), 0)
        hot_ref[d * rows : (d + 1) * rows, :] = hot
        marked = hot * docs
        slot_docs = marked[:, :128]
        for i in range(128, routes, 128):
            slot_docs = slot_docs + marked[:, i : i + 128]
        slot_docs = jnp.sum(slot_docs.astype(jnp.float32), axis=1, keepdims=True)
        table = jnp.zeros((CAP, DOC_LANES), jnp.float32)
        for h in range(count):
            table = jnp.where(lane == h, slot_docs[h * CAP : (h + 1) * CAP], table)
        thirds = [table[i * DOC_ROWS : (i + 1) * DOC_ROWS] for i in range(CAP // DOC_ROWS)]
        packed = jnp.concatenate(thirds + [jnp.zeros_like(thirds[0])], 1)
        blank = jnp.zeros((DOC_ROWS, head_size), jnp.float32)
        out_ref[rows:, :] = jnp.concatenate([blank, packed, blank], 1).astype(jnp.bfloat16)
    taken = dot(hot_ref[...], rows_ref[...], NN).astype(jnp.bfloat16)
    for d, out_ref in enumerate(out_refs):
        out_ref[:rows, :] = taken[d * rows : (d + 1) * rows]


def doc_table(packed):
    packed = packed.astype(jnp.float32)
    thirds = [packed[:, i * DOC_LANES : (i + 1) * DOC_LANES] for i in range(CAP // DOC_ROWS)]
    return jnp.concatenate(thirds, 0)


def attention_kernel(count, groups, *refs):
    blocks = refs[:groups]
    before_ref = refs[groups]
    near_ref, far_ref, own_ref, mask_ref = refs[groups + 1 :]
    me = lax.axis_index("head")
    rows = count * CAP
    head_size = blocks[0].shape[1] // 4
    scaling = head_size ** (-0.5)
    span = groups * CAP
    query_docs = jnp.concatenate(
        [doc_table(b[rows:, head_size : 3 * head_size]) for b in blocks], 0
    )
    before_docs = jnp.concatenate([doc_table(before_ref[d, rows:, :]) for d in range(groups)], 0)
    key_docs = jnp.concatenate([before_docs, query_docs], 0)
    key_docs = jnp.concatenate([key_docs, jnp.zeros_like(key_docs)], 1).T

    def order(index):
        return (me ^ (index // CAP)) * CAP + index % CAP

    row_order = order(lax.broadcasted_iota(jnp.int32, (span, 1), 0))
    column = lax.broadcasted_iota(jnp.int32, (1, 2 * span), 1)
    column_order = jnp.where(column < span, -1, order(jnp.maximum(column - span, 0)))
    mask_ref[...] = jnp.where(column_order <= row_order, 0.0, MASKED)

    def piece(h, i):
        here, part = slice(h * CAP, (h + 1) * CAP), slice(i * head_size, (i + 1) * head_size)
        return jnp.concatenate([b[here, part] for b in blocks], 0)

    def both(h, i):
        here, part = slice(h * CAP, (h + 1) * CAP), slice(i * head_size, (i + 1) * head_size)
        earlier = [before_ref[d, here, part] for d in range(groups)]
        return jnp.concatenate(earlier + [piece(h, i + 1)], 0)

    for start in range(0, count, TOGETHER):
        heads = range(start, min(start + TOGETHER, count))
        queries = [piece(h, 0) for h in heads]
        grads_out = [piece(h, 3) for h in heads]
        key_rows = [both(h, 0) for h in heads]
        value_rows = [both(h, 1) for h in heads]
        scores = [dot(q, k, NT) for q, k in zip(queries, key_rows)]
        weight_grads = [dot(g, v, NT) for g, v in zip(grads_out, value_rows)]
        weights = []
        for h, s in zip(heads, scores):
            s = s * scaling + mask_ref[...]
            s = jnp.where(key_docs[h : h + 1, :] == query_docs[:, h : h + 1], s, MASKED)
            powers = jnp.exp(s - jnp.max(s, axis=1, keepdims=True))
            weights.append(powers * (1.0 / jnp.sum(powers, axis=1, keepdims=True)))
        weights_low = [w.astype(jnp.bfloat16) for w in weights]
        attended = [dot(w, v, NN).astype(jnp.bfloat16) for w, v in zip(weights_low, value_rows)]
        value_grads = [dot(w, g, TN) for w, g in zip(weights_low, grads_out)]
        deltas = [
            jnp.sum(g.astype(jnp.float32) * a.astype(jnp.float32), axis=1, keepdims=True)
            for g, a in zip(grads_out, attended)
        ]
        score_grads = [
            (w * (wg - d)).astype(jnp.bfloat16) for w, wg, d in zip(weights, weight_grads, deltas)
        ]
        query_grads = [
            (dot(s, k, NN) * scaling).astype(jnp.bfloat16) for s, k in zip(score_grads, key_rows)
        ]
        key_grads = [dot(s, q, TN) * scaling for s, q in zip(score_grads, queries)]
        for i, h in enumerate(heads):
            here = slice(h * CAP, (h + 1) * CAP)
            for d in range(groups):
                part = slice(d * CAP, (d + 1) * CAP)
                own = slice(span + d * CAP, span + (d + 1) * CAP)
                near_ref[d, here, :head_size] = attended[i][part]
                near_ref[d, here, head_size:] = query_grads[i][part]
                far_ref[d, here, :head_size] = key_grads[i][part].astype(jnp.bfloat16)
                far_ref[d, here, head_size:] = value_grads[i][part].astype(jnp.bfloat16)
                own_ref[d, here, :head_size] = key_grads[i][own]
                own_ref[d, here, head_size:] = value_grads[i][own]


def combine_kernel(groups, near_ref, own_ref, incoming_ref, *out_refs):
    half = near_ref.shape[2]
    for d in range(groups):
        out_refs[d][:, :half] = near_ref[d]
        total = own_ref[d] + incoming_ref[d].astype(jnp.float32)
        out_refs[d][:, half:] = total.astype(jnp.bfloat16)


def routed(first, count, owned, groups, refs):
    column_ref = refs[0]
    blocks = refs[1 : groups + 1]
    hot_ref = refs[-1]
    me = lax.axis_index("head")
    rows = count * CAP
    routes = column_ref.shape[0]
    for d in range(groups):
        base = ((me ^ d) * owned + first) * CAP
        hot = one_hot(column_ref[:, 0:1], base, rows, (routes, rows), 1)
        hot_ref[:, d * rows : (d + 1) * rows] = hot
    return dot(hot_ref[...], jnp.concatenate([b[...] for b in blocks], 0), NN)


def return_kernel(first, count, owned, groups, initial, *refs):
    taken = routed(first, count, owned, groups, refs)
    if not initial:
        taken = taken + refs[groups + 1][...].astype(jnp.float32)
    refs[-2][...] = taken.astype(jnp.bfloat16)


def finish_kernel(first, count, owned, groups, initial, *refs):
    logits_ref, cot_ref, heads_out_ref, proj_grads_ref, gate_grads_ref = refs[-6:-1]
    taken = routed(first, count, owned, groups, refs)
    if not initial:
        taken = taken + refs[groups + 1][...].astype(jnp.float32)
    head_size = cot_ref.shape[1]
    top, tokens = logits_ref.shape
    routes = tokens * top
    proj_grads_ref[...] = taken[:, head_size:].astype(jnp.bfloat16)
    attended = taken[:, :head_size]
    gate_table = sigmoid(logits_ref[...])
    heads_out_ref[...] = (attended * route_column(gate_table)).astype(jnp.bfloat16)
    sums = jnp.sum(cot_ref[...].astype(jnp.float32) * attended, axis=1, keepdims=True)
    sums = jnp.where(own_route(routes, top), sums, 0.0).reshape(tokens, top, top)
    gate_grads_ref[...] = jnp.sum(sums, axis=1).T * gate_table * (1.0 - gate_table)


def shifted(block, axis, distance):
    devices = range(lax.axis_size(axis))
    route = [(i, i + distance) for i in devices if i + distance in devices]
    return lax.ppermute(block, axis, route)


def exchanged(blocks):
    groups = len(blocks)
    return [blocks[0]] + [
        lax.ppermute(blocks[d], "head", [(i, i ^ d) for i in range(groups)])
        for d in range(1, groups)
    ]


def per_device(projections, routed_heads, slot_index, gate_logits, doc_lengths, cotangent):
    tokens, top, width = projections.shape
    head_size = width // 3
    routes = tokens * top
    groups = lax.axis_size("head")
    owned = H // groups
    bf16, f32 = jnp.bfloat16, jnp.float32

    shape = jax.ShapeDtypeStruct
    logits = gate_logits.T
    cot_rows = cotangent.reshape(routes, head_size)
    chunks = head_chunks(owned)
    last = len(chunks) - 1

    def sent_shapes(count):
        return [shape((count * CAP + DOC_ROWS, width + head_size), bf16)] * groups

    def hot_scratch(count):
        return pltpu.VMEM((groups * count * CAP, routes), bf16)

    flat, columns, documents, rows_in, *sent = call(
        partial(prepare_kernel, *chunks[0], owned, groups),
        [
            shape((8, routes), jnp.int32),
            shape((routes, 128), jnp.int32),
            shape((8, routes), f32),
            shape((routes, width + head_size), bf16),
        ]
        + sent_shapes(chunks[0][1]),
        routed_heads.T,
        slot_index.T,
        logits,
        doc_lengths,
        projections.reshape(routes, width),
        cot_rows,
        in_specs=[ANY] * 3 + [pl.BlockSpec(memory_space=pltpu.SMEM)] + [ANY] * 2,
        scratch=[
            pltpu.VMEM((top, tokens), jnp.int32),
            pltpu.VMEM((top, tokens), jnp.int32),
            pltpu.VMEM((top, tokens), f32),
            pltpu.VMEM((routes, width), bf16),
            pltpu.VMEM((routes, head_size), bf16),
            hot_scratch(chunks[0][1]),
            pltpu.SemaphoreType.DMA((5,)),
        ],
        limit=PREPARE_BYTES,
        cost=COSTS[0],
    )
    blocks_out = [sent]
    for first, count in chunks[1:]:
        sent = call(
            partial(dispatch_kernel, first, count, owned, groups),
            sent_shapes(count),
            flat,
            documents,
            rows_in,
            scratch=[hot_scratch(count)],
            cost=COSTS[0],
        )
        blocks_out.append(sent)
    received = []
    for i, sent in enumerate(blocks_out):
        with jax.named_scope(f"send_out_{i}"):
            received.append(exchanged(sent))

    homes, fars, returned = [], [], []
    for i, ((first, count), blocks) in enumerate(zip(chunks, received)):
        rows = count * CAP
        if i > 0:
            *blocks, _ = lax.optimization_barrier((*blocks, fars[-1]))
        else:
            waits = [sent[0] for sent in blocks_out[1:]]
            blocks = lax.optimization_barrier((*blocks, *waits))[: len(blocks)]
        with jax.named_scope(f"send_next_{i}"):
            before = shifted(jnp.stack([b[:, head_size : 3 * head_size] for b in blocks]), "seq", 1)
        if i > 0:
            homes.append(finish_chunk(incoming))
            with jax.named_scope(f"send_home_{i - 1}"):
                returned.append(exchanged(homes[-1]))
        pair = (groups, rows, 2 * head_size)
        near, far, own = call(
            partial(attention_kernel, count, groups),
            [shape(pair, bf16), shape(pair, bf16), shape(pair, f32)],
            *blocks,
            before,
            after=[homes[-1][0]] if homes else (),
            scratch=[pltpu.VMEM((groups * CAP, 2 * groups * CAP), f32)],
            pairs=2 * (groups * CAP) ** 2,
            cost=COSTS[1],
        )
        fars.append(far)

        with jax.named_scope(f"send_back_{i}"):
            incoming = shifted(far, "seq", -1)

        def finish_chunk(incoming, near=near, own=own, rows=rows):
            return call(
                partial(combine_kernel, groups),
                [shape((rows, 4 * head_size), bf16)] * groups,
                near,
                own,
                incoming,
                cost=COSTS[2],
            )

    homes.append(finish_chunk(incoming))
    with jax.named_scope(f"send_home_{last}"):
        returned.append(exchanged(homes[-1]))
    total = []
    for i, ((first, count), home) in enumerate(zip(chunks, homes)):
        rows = count * CAP
        operands = [columns, *returned[i], *total]
        scratch = [pltpu.VMEM((routes, groups * rows), bf16)]
        if i < last:
            total = [
                call(
                    partial(return_kernel, first, count, owned, groups, i == 0),
                    shape((routes, 4 * head_size), bf16),
                    *operands,
                    after=[homes[i + 1][0]],
                    scratch=scratch,
                    cost=COSTS[3],
                )
            ]
    head_outputs, projection_grads, gate_grads = call(
        partial(finish_kernel, first, count, owned, groups, last == 0),
        [
            shape((routes, head_size), bf16),
            shape((routes, width), bf16),
            shape(logits.shape, f32),
        ],
        *operands,
        logits,
        cot_rows,
        scratch=scratch,
    )
    return (
        head_outputs.reshape(tokens, top, head_size),
        projection_grads.reshape(tokens, top, width),
        gate_grads.T,
    )


def solution(mesh):
    return jax.shard_map(
        per_device,
        mesh=mesh,
        in_specs=(
            P(("seq", "head"), None, None),
            P(("seq", "head"), None),
            P(("seq", "head"), None),
            P(("seq", "head"), None),
            P(),
            P(("seq", "head"), None, None),
        ),
        out_specs=(
            P(("seq", "head"), None, None),
            P(("seq", "head"), None, None),
            P(("seq", "head"), None),
        ),
        check_vma=False,
    )
```
